512 devices in a mesh: rows: 16 (over x, z_hi), cols: 32 (over z_lo, y, core).
Axes of the slice: x: 4, y: 8, z: 8 (z_hi: 4, z_lo: 2; z = z_hi * 2 + z_lo), core: 2. Of those that a mesh axis runs over, the one named last changes fastest.
Arguments:
- coefficients: float32 [1024, 8192], P('cols', 'rows'), may hold values from -6 to 6
- factor_panel: float32 [8192, 1024], P('rows'), may hold values from -0.0625 to 0.0625
- block_inverse: float32 [8192, 512], P('rows'), may hold values from -0.044194174 to 2, as said below
- train_inputs: float32 [14, 8192], P(None, 'rows'), may hold values from 0 to 1
- query_points: float32 [14, 8192], replicated, may hold values from 0 to 1
- inv_length: float32 [14], replicated, may hold values from 0.25 to 2
- amplitude: float32 [1024], P('cols'), may hold values from 0.02 to 0.2
Outputs:
- weights: float32 [1024, 8192], P('cols', 'rows')
- predicted_mean: float32 [1024, 8192], P('cols', 'rows')
The draws below stay inside these ranges and needn't reach their ends.
Inputs may be any that keep to these rules, and one draw needn't show every extreme that they name: `block_inverse`: each block of 512 rows is lower triangular, with diagonal entries from 1 to 2.
All inputs are finite; a program needn't handle non-finite values.
Results may differ from the reference program's by a relative error of at most 0.004.
Values may be sent and summed in bfloat16 or wider, within the bound.
No kernel may reach another device: no remote copies, remote signals or barrier semaphores. Data moves between devices by JAX's collectives and lax.ppermute only.
A program may use at most 64 MiB of HBM per device.

```python
import math
import jax
import jax.numpy as jnp
from jax import lax

M = 1024
PARAMS = 14
BLK = 512
QRY = 8192
N_TRAIN = 8192


def draw_block_inverse(key, part):
    first_key, second_key = jax.random.split(key)
    row_ids = (jnp.arange(N_TRAIN) % BLK)[:, None]
    col_ids = jnp.arange(BLK)[None, :]
    below = jax.random.uniform(first_key, (N_TRAIN, BLK), jnp.float32, -1.0, 1.0) * BLK ** (-0.5)
    on_diag = jax.random.uniform(second_key, (N_TRAIN, BLK), jnp.float32, 1.0, 2.0)
    return jnp.where(col_ids == row_ids, on_diag, jnp.where(col_ids < row_ids, below, 0.0))


def block_scale(own_key, extent, shards, smallest, top_value):
    def one(axis_at, blocks):
        draws = jax.random.uniform(jax.random.fold_in(jax.random.fold_in(own_key, 6), axis_at), (blocks,), jnp.float32, smallest / len(shards), top_value / len(shards))
        return jnp.repeat(jnp.exp(draws), extent[axis_at] // blocks).reshape((-1,) + (1,) * (len(extent) - axis_at - 1))

    gain = one(*shards[0])
    for cut in shards[1:]:
        gain = gain * one(*cut)
    return gain


def normal_values(stream_key, shape, deviation, most, shards=(), kind=jnp.bfloat16):
    gain = block_scale(stream_key, shape, shards, -0.22, 0.18) if shards else 1.0
    entries = jax.random.normal(stream_key, shape, jnp.float32) * deviation * gain
    return jnp.minimum(jnp.maximum(entries, -most), most).astype(kind)


def setup_inputs(seed: int = 0) -> dict:
    key_list = jax.random.split(jax.random.key(seed), 8)
    return {
        "coefficients": normal_values(key_list[0], (M, N_TRAIN), 1.0, 6.0, ((0, 32), (1, 16)), jnp.float32),
        "factor_panel": normal_values(key_list[1], (N_TRAIN, 2 * BLK), N_TRAIN ** -0.5, 0.0625, ((0, 16),), jnp.float32),
        "block_inverse": draw_block_inverse(jax.random.fold_in(key_list[7], 71), 0),
        "train_inputs": jnp.clip(1.0 * jax.random.uniform(key_list[3], (PARAMS, N_TRAIN), jnp.float32) ** block_scale(key_list[3], (PARAMS, N_TRAIN), ((1, 16),), -0.2, 0.2), 0.0, 1.0),
        "query_points": jnp.clip(jax.random.uniform(key_list[4], (PARAMS, QRY), jnp.float32, 0.0, 1.0), 0.0, 1.0),
        "inv_length": jnp.clip(jnp.exp(jax.random.uniform(key_list[5], (PARAMS,), jnp.float32, math.log(0.25), math.log(2.0))), 0.25, 2.0),
        "amplitude": jnp.clip(jnp.exp(math.log(0.2) - 2.3025851 * jax.random.uniform(key_list[6], (M,), jnp.float32) ** block_scale(key_list[6], (M,), ((0, 32),), -0.2, 0.2)), 0.02, 0.2),
    }


def kernel_values(train_part, query_part, inv_length):
    squared = jnp.zeros((train_part.shape[1], query_part.shape[1]), jnp.float32)
    for dim_index in range(train_part.shape[0]):
        offset = (train_part[dim_index][:, None] - query_part[dim_index][None, :]) * inv_length[dim_index]
        squared = squared + offset * offset
    return jnp.exp(-jnp.sqrt(squared + 1e-06)).astype(jnp.bfloat16)

def solve_product(left, right):
    return jnp.dot(left, right, precision=lax.Precision.HIGHEST, preferred_element_type=jnp.float32)

def reference(coefficients, factor_panel, block_inverse, train_inputs, query_points, inv_length, amplitude):
    block_len = BLK
    solved_rest = coefficients[:, 2 * block_len:]
    rest_one = solve_product(solved_rest, factor_panel[2 * block_len:, block_len:])
    weights_one = solve_product(coefficients[:, block_len:2 * block_len] - rest_one, block_inverse[block_len:2 * block_len])
    rest_zero = solve_product(solved_rest, factor_panel[2 * block_len:, :block_len]) + solve_product(weights_one, factor_panel[block_len:2 * block_len, :block_len])
    weights_zero = solve_product(coefficients[:, :block_len] - rest_zero, block_inverse[:block_len])
    weights = jnp.concatenate([weights_zero, weights_one, solved_rest], axis=1)
    weights_low = weights.astype(jnp.bfloat16)
    span_len = math.gcd(QRY, 512)
    span_count = QRY // span_len
    grouped = query_points.reshape(PARAMS, span_count, span_len).transpose(1, 0, 2)

    def predict_block(query_block):
        return jnp.dot(weights_low, kernel_values(train_inputs, query_block, inv_length), preferred_element_type=jnp.float32)
    blocks_out = lax.map(predict_block, grouped)
    predicted_mean = blocks_out.transpose(1, 0, 2).reshape(M, QRY) * amplitude[:, None]
    return (weights, predicted_mean)
```

```python
import math

import jax
import jax.numpy as jnp
from jax import lax
from jax.experimental import pallas as pl
from jax.experimental.pallas import tpu as pltpu
from jax.sharding import PartitionSpec as P

F32 = jnp.float32
BF16 = jnp.bfloat16
LOG2E = math.log2(math.e)
FLOOR = 1e-06 * LOG2E * LOG2E


def three_pieces(values):
    high = values.astype(BF16).astype(F32)
    rest = values - high
    middle = rest.astype(BF16).astype(F32)
    low = (rest - middle).astype(BF16).astype(F32)
    return high, middle, low


def extra_rows(rows, count):
    width = rows[0].shape[1]
    index = lax.broadcasted_iota(jnp.int32, (count, width), 0)
    block = jnp.zeros((count, width), F32)
    for place, row in enumerate(rows):
        block = jnp.where(index == place, jnp.broadcast_to(row, (count, width)), block)
    return block


def train_side(points):
    norm = jnp.sum(points * points, axis=0, keepdims=True)
    high, middle, low = (-2.0 * piece for piece in three_pieces(points))
    one = jnp.ones_like(norm)
    extra = extra_rows([one, one, one, *three_pieces(norm)], 32)
    return jnp.concatenate([high, middle, low, high, middle, high, extra], axis=0)


def query_side(points):
    norm = jnp.sum(points * points, axis=0, keepdims=True)
    high, middle, low = three_pieces(points)
    one = jnp.ones_like(norm)
    extra = extra_rows([*three_pieces(norm), one, one, one], 32)
    return jnp.concatenate([high, high, high, middle, middle, low, extra], axis=0)


def kernel_block(train_ref, query_ref, scale_ref, out_ref, left_ref):
    scale = scale_ref[...]

    @pl.when(pl.program_id(0) == 0)
    def _():
        left = train_side((train_ref[...] - 0.5) * scale)
        left_ref[...] = left.T.astype(BF16)

    right = query_side((query_ref[...] - 0.5) * scale).astype(BF16)
    squared = jnp.dot(left_ref[...], right, preferred_element_type=F32)
    squared = jnp.maximum(squared, 0.0) + FLOOR
    out_ref[0] = jnp.exp2(-(squared * lax.rsqrt(squared))).astype(BF16)


def kernel_values(train_inputs, query_points, inv_length, piece):
    params, plans = train_inputs.shape
    queries = query_points.shape[1]
    count = queries // piece
    spare = ((0, 16 - params), (0, 0))
    scale = jnp.pad((inv_length * LOG2E)[:, None], spare)
    return pl.pallas_call(
        kernel_block,
        out_shape=jax.ShapeDtypeStruct((count, plans, piece), BF16),
        grid=(count,),
        in_specs=[
            pl.BlockSpec((16, plans), lambda j: (0, 0)),
            pl.BlockSpec((16, piece), lambda j: (0, j)),
            pl.BlockSpec((16, 1), lambda j: (0, 0)),
        ],
        out_specs=pl.BlockSpec((1, plans, piece), lambda j: (j, 0, 0)),
        scratch_shapes=[pltpu.VMEM((plans, 128), BF16)],
        compiler_params=pltpu.CompilerParams(vmem_limit_bytes=32 * 1024 * 1024),
        cost_estimate=pl.CostEstimate(
            flops=2 * 128 * plans * queries,
            bytes_accessed=2 * plans * queries,
            transcendentals=2 * plans * queries,
        ),
        name="kernel_values",
    )(jnp.pad(train_inputs, spare), jnp.pad(query_points, spare), scale)


def predict_block(weights_ref, kernel_ref, out_ref):
    out_ref[0] = jnp.dot(
        weights_ref[...], kernel_ref[0], preferred_element_type=F32
    ).astype(BF16)


def predictions(weights_low, kernel):
    count, plans, piece = kernel.shape
    rows = weights_low.shape[0]
    return pl.pallas_call(
        predict_block,
        out_shape=jax.ShapeDtypeStruct((count, rows, piece), BF16),
        grid=(count,),
        in_specs=[
            pl.BlockSpec((rows, plans), lambda j: (0, 0)),
            pl.BlockSpec((1, plans, piece), lambda j: (j, 0, 0)),
        ],
        out_specs=pl.BlockSpec((1, rows, piece), lambda j: (j, 0, 0)),
        cost_estimate=pl.CostEstimate(
            flops=2 * rows * plans * piece * count,
            bytes_accessed=2 * plans * piece * count,
            transcendentals=0,
        ),
        name="predictions",
    )(weights_low, kernel)


def product(left, right):
    return jnp.dot(left, right, precision=lax.Precision.HIGH, preferred_element_type=F32)


def on_device(
    coefficients, factor_panel, block_inverse, train_inputs, query_points, inv_length, amplitude
):
    rows, block_len = coefficients.shape
    row_index = lax.axis_index("rows")
    row_count = lax.axis_size("rows")

    partial = jnp.where(row_index >= 2, product(coefficients, factor_panel), 0.0).astype(BF16)
    slots = jnp.concatenate(
        [
            partial[None, :, :block_len],
            partial[None, :, block_len:],
            jnp.zeros((row_count - 2, rows, block_len), BF16),
        ]
    )
    arrived = lax.all_to_all(slots, "rows", 0, 0, tiled=True)
    right_side = coefficients - jnp.sum(arrived.astype(F32), axis=0)
    solved = product(right_side, block_inverse)
    carried = product(solved, factor_panel[:, :block_len])
    carried = lax.ppermute(carried, "rows", [(1, 0)])
    solved = solved - product(carried, block_inverse)
    weights = jnp.where(row_index < 2, solved, coefficients)

    kernel = kernel_values(
        train_inputs, query_points, inv_length, query_points.shape[1] // row_count
    )
    pieces = predictions(weights.astype(BF16), kernel)
    pieces = lax.all_to_all(pieces, "rows", 0, 0, tiled=True)
    predicted_mean = jnp.sum(pieces.astype(F32), axis=0) * amplitude[:, None]
    return (weights, predicted_mean)


def solution(mesh):
    return jax.shard_map(
        on_device,
        mesh=mesh,
        in_specs=(
            P("cols", "rows"),
            P("rows", None),
            P("rows", None),
            P(None, "rows"),
            P(),
            P(),
            P("cols"),
        ),
        out_specs=(P("cols", "rows"), P("cols", "rows")),
        check_vma=False,
    )
```

```python
import functools
import math

import jax
import jax.numpy as jnp
from jax import lax
from jax.experimental import pallas as pl
from jax.experimental.pallas import tpu as pltpu
from jax.sharding import PartitionSpec as P

F32 = jnp.float32
BF16 = jnp.bfloat16
LOG2E = math.log2(math.e)
FLOOR = 1e-06 * LOG2E * LOG2E
PADDED = 16
WHOLE = pl.BlockSpec(memory_space=pltpu.VMEM)
SCALARS = pl.BlockSpec(memory_space=pltpu.SMEM)
UNREAD = pl.BlockSpec(memory_space=pl.ANY)
PARAMS = pltpu.CompilerParams(vmem_limit_bytes=16 * 1024 * 1024)

def split(values):
    high = values.astype(BF16)
    return high, (values - high.astype(F32)).astype(BF16)


def dot(left, right):
    return jnp.dot(left, right, preferred_element_type=F32)


def product(left, right_high, right_low):
    rows = left.shape[0]
    left_high, left_low = split(left)
    both = dot(jnp.concatenate([left_high, left_low], axis=0), right_high)
    return both[:rows] + both[rows:] + dot(left_high, right_low)


def three_pieces(values):
    high = values.astype(BF16).astype(F32)
    rest = values - high
    middle = rest.astype(BF16).astype(F32)
    low = (rest - middle).astype(BF16).astype(F32)
    return high, middle, low


def extra_rows(rows, count):
    width = rows[0].shape[1]
    index = lax.broadcasted_iota(jnp.int32, (count, width), 0)
    block = jnp.zeros((count, width), F32)
    for place, row in enumerate(rows):
        block = jnp.where(index == place, jnp.broadcast_to(row, (count, width)), block)
    return block


def train_side(points):
    norm = jnp.sum(points * points, axis=0, keepdims=True)
    high, middle, low = (-2.0 * piece for piece in three_pieces(points))
    one = jnp.ones_like(norm)
    extra = extra_rows([one, one, one, *three_pieces(norm)], 32)
    left = jnp.concatenate([high, middle, low, high, middle, high, extra], axis=0)
    return left.T.astype(BF16)


def query_side(points):
    norm = jnp.sum(points * points, axis=0, keepdims=True)
    high, middle, low = three_pieces(points)
    one = jnp.ones_like(norm)
    extra = extra_rows([*three_pieces(norm), one, one, one], 32)
    right = jnp.concatenate([high, high, high, middle, middle, low, extra], axis=0)
    return right.astype(BF16)


def kernel_values(left, right):
    squared = jnp.maximum(dot(left, right), 0.0) + FLOOR
    return jnp.exp2(-(squared * lax.rsqrt(squared))).astype(BF16)


def scale_column(inv_length_ref):
    index = lax.broadcasted_iota(jnp.int32, (PADDED, 1), 0)
    column = jnp.zeros((PADDED, 1), F32)
    for place in range(inv_length_ref.shape[0]):
        column = jnp.where(index == place, inv_length_ref[place] * LOG2E, column)
    return column


def centred(pad_ref, points):
    pad_ref[...] = jnp.zeros_like(pad_ref)
    pad_ref[: points.shape[0], :] = points - 0.5
    return pad_ref[...]


def residual_kernel(coefficients_ref, factor_ref, train_ref, out_ref, pad_ref):
    row_index = lax.axis_index("rows")
    step = pl.program_id(0)
    width = factor_ref.shape[1]
    parts = out_ref.shape[2] // width

    @pl.when((row_index >= 2) & (step == 0))
    def _():
        out_ref[...] = jnp.zeros_like(out_ref)

    for place in range(2 * parts):
        columns = slice(place % parts * width, (place % parts + 1) * width)

        @pl.when((row_index >= 2) & (step == place))
        def _():
            partial = product(coefficients_ref[...], *split(factor_ref[...]))
            out_ref[place // parts, :, columns] = partial.astype(BF16)

        @pl.when((row_index < 2) & (step == place))
        def _():
            if place < parts:
                both = jnp.concatenate(split(centred(pad_ref, train_ref[...])), axis=0)
                for slot in range(out_ref.shape[0]):
                    out_ref[slot, :, columns] = both


def residuals(coefficients, factor_panel, train_inputs, row_count):
    rows, block_len = coefficients.shape
    width = block_len // 2
    return pl.pallas_call(
        residual_kernel,
        out_shape=jax.ShapeDtypeStruct((row_count, rows, block_len), BF16),
        grid=(4,),
        in_specs=[
            pl.BlockSpec((rows, block_len), lambda j: (0, 0)),
            pl.BlockSpec((block_len, width), lambda j: (0, j)),
            pl.BlockSpec((train_inputs.shape[0], width), lambda j: (0, jnp.minimum(j, 1))),
        ],
        out_specs=pl.BlockSpec((row_count, rows, block_len), lambda j: (0, 0, 0)),
        scratch_shapes=[pltpu.VMEM((PADDED, width), F32)],
        compiler_params=PARAMS,
        name="residuals",
    )(coefficients, factor_panel, train_inputs)


def own_kernel(
    coefficients_ref, train_ref, query_ref, inv_length_ref, inverse_ref, factor_ref,
    out_ref, inverse_high_ref, inverse_low_ref, factor_high_ref, factor_low_ref,
    left_ref, pad_ref, pad_query_ref, stage_ref, sems,
):
    row_index = lax.axis_index("rows")
    count, _, piece = out_ref.shape

    @pl.when(row_index < 2)
    def _():
        width = stage_ref.shape[2]
        copies = [
            pltpu.make_async_copy(inverse_ref, stage_ref.at[0], sems.at[0]),
            pltpu.make_async_copy(factor_ref.at[:, :width], stage_ref.at[1], sems.at[1]),
        ]
        for copy in copies:
            copy.start()
        out_ref[...] = jnp.zeros_like(out_ref)
        for copy in copies:
            copy.wait()
        inverse_high_ref[...], inverse_low_ref[...] = split(stage_ref[0])
        factor_high_ref[...], factor_low_ref[...] = split(stage_ref[1])

    @pl.when(row_index >= 2)
    def _():
        scale = scale_column(inv_length_ref)
        left_ref[...] = train_side(centred(pad_ref, train_ref[...]) * scale)
        low = coefficients_ref[...].astype(BF16)

        def step(place, carry):
            chosen = query_ref[:, pl.ds(pl.multiple_of(place * piece, piece), piece)]
            right = query_side(centred(pad_query_ref, chosen) * scale)
            out_ref[place] = dot(low, kernel_values(left_ref[...], right)).astype(BF16)
            return carry

        lax.fori_loop(0, count, step, 0)


def own_work(coefficients, train_inputs, query_points, inv_length, block_inverse, factor_panel, row_count):
    rows, plans = coefficients.shape
    queries = query_points.shape[1]
    piece = queries // row_count
    square = jax.ShapeDtypeStruct(block_inverse.shape, BF16)
    return pl.pallas_call(
        own_kernel,
        out_shape=(jax.ShapeDtypeStruct((row_count, rows, piece), BF16),) + (square,) * 4,
        in_specs=[WHOLE, WHOLE, WHOLE, SCALARS, UNREAD, UNREAD],
        out_specs=(WHOLE,) * 5,
        scratch_shapes=[
            pltpu.VMEM((plans, 128), BF16),
            pltpu.VMEM((PADDED, plans), F32),
            pltpu.VMEM((PADDED, piece), F32),
            pltpu.VMEM((2, *block_inverse.shape), F32),
            pltpu.SemaphoreType.DMA((2,)),
        ],
        compiler_params=PARAMS,
        cost_estimate=pl.CostEstimate(
            flops=2 * 160 * plans * queries, bytes_accessed=1 << 20, transcendentals=2 * plans * queries
        ),
        name="own_work",
    )(coefficients, train_inputs, query_points, inv_length, block_inverse, factor_panel)


def solve_kernel(
    coefficients_ref, arrived_ref, inverse_high_ref, inverse_low_ref, factor_high_ref, factor_low_ref, out_ref, send_ref
):
    row_index = lax.axis_index("rows")

    @pl.when(row_index < 2)
    def _():
        total = jnp.sum(arrived_ref[2:].astype(F32), axis=0)
        out_ref[...] = product(coefficients_ref[...] - total, inverse_high_ref[...], inverse_low_ref[...])

    @pl.when(row_index == 1)
    def _():
        send_ref[...] = product(out_ref[...], factor_high_ref[...], factor_low_ref[...]).astype(BF16)

    @pl.when(row_index != 1)
    def _():
        send_ref[...] = jnp.zeros_like(send_ref)

    @pl.when(row_index >= 2)
    def _():
        out_ref[...] = coefficients_ref[...]


def solve(coefficients, arrived, squares):
    rows, block_len = coefficients.shape
    return pl.pallas_call(
        solve_kernel,
        out_shape=(
            jax.ShapeDtypeStruct((rows, block_len), F32),
            jax.ShapeDtypeStruct((rows, block_len), BF16),
        ),
        in_specs=[WHOLE] * 6,
        out_specs=(WHOLE, WHOLE),
        compiler_params=PARAMS,
        name="solve",
    )(coefficients, arrived, *squares)


def near_kernel(arrived_ref, query_ref, inv_length_ref, _, kernel_ref, pad_ref):
    scale = scale_column(inv_length_ref)
    right = query_side(centred(pad_ref, query_ref[...]) * scale)
    plans = arrived_ref.shape[2]
    for block in range(2):
        both = arrived_ref[block].astype(F32)
        left = train_side((both[:PADDED] + both[PADDED:]) * scale)
        kernel_ref[block * plans : (block + 1) * plans, :] = kernel_values(left, right)


def near(arrived, own_queries, inv_length, unread):
    plans, queries = arrived.shape[2], own_queries.shape[1]
    return pl.pallas_call(
        near_kernel,
        out_shape=jax.ShapeDtypeStruct((2 * plans, queries), BF16),
        in_specs=[WHOLE, WHOLE, SCALARS, UNREAD],
        out_specs=WHOLE,
        scratch_shapes=[pltpu.VMEM((PADDED, queries), F32)],
        compiler_params=PARAMS,
        cost_estimate=pl.CostEstimate(
            flops=4 * 128 * plans * queries, bytes_accessed=1 << 20, transcendentals=4 * plans * queries
        ),
        name="near",
    )(arrived, own_queries, inv_length, unread)


def correct_kernel(solved_ref, carried_ref, inverse_high_ref, inverse_low_ref, _, __, out_ref, slots_ref, low_ref, sems):
    row_index = lax.axis_index("rows")

    @pl.when(row_index == 0)
    def _():
        carried = carried_ref[...]
        out_ref[...] = solved_ref[...] - (dot(carried, inverse_high_ref[...]) + dot(carried, inverse_low_ref[...]))

    @pl.when(row_index > 0)
    def _():
        out_ref[...] = solved_ref[...]

    @pl.when(row_index < 2)
    def _():
        low_ref[...] = out_ref[...].astype(BF16)
        copies = [
            pltpu.make_async_copy(low_ref, slots_ref.at[slot], sems.at[slot])
            for slot in range(slots_ref.shape[0])
        ]
        for copy in copies:
            copy.start()
        for copy in copies:
            copy.wait()


def correct(solved, carried, inverse_high, inverse_low, slots, unread):
    return pl.pallas_call(
        correct_kernel,
        out_shape=(
            jax.ShapeDtypeStruct(solved.shape, F32),
            jax.ShapeDtypeStruct(slots.shape, slots.dtype),
        ),
        in_specs=[WHOLE] * 4 + [UNREAD] * 2,
        out_specs=(WHOLE, UNREAD),
        input_output_aliases={4: 1},
        scratch_shapes=[
            pltpu.VMEM(solved.shape, BF16),
            pltpu.SemaphoreType.DMA((slots.shape[0],)),
        ],
        compiler_params=PARAMS,
        name="correct",
    )(solved, carried, inverse_high, inverse_low, slots, unread)


def finish_kernel(pieces_ref, kernel_ref, amplitude_ref, mean_ref):
    rows = mean_ref.shape[0]
    plans = kernel_ref.shape[0] // 2
    mean = jnp.sum(pieces_ref[2:].astype(F32), axis=0)
    mean = mean + dot(pieces_ref[0], kernel_ref[:plans, :]) + dot(pieces_ref[1], kernel_ref[plans:, :])
    index = lax.broadcasted_iota(jnp.int32, (rows, 1), 0)
    amplitude = jnp.zeros((rows, 1), F32)
    for row in range(rows):
        amplitude = jnp.where(index == row, amplitude_ref[row], amplitude)
    mean_ref[...] = mean * amplitude


def finish(pieces, kernel, amplitude):
    return pl.pallas_call(
        finish_kernel,
        out_shape=jax.ShapeDtypeStruct(pieces.shape[1:], F32),
        in_specs=[WHOLE, WHOLE, SCALARS],
        out_specs=WHOLE,
        compiler_params=PARAMS,
        name="finish",
    )(pieces, kernel, amplitude)


def on_device(
    coefficients, factor_panel, block_inverse, train_inputs, query_points, inv_length, amplitude
):
    row_index = lax.axis_index("rows")
    row_count = lax.axis_size("rows")
    piece = query_points.shape[1] // row_count

    slots = residuals(coefficients, factor_panel, train_inputs, row_count)
    arrived = lax.all_to_all(slots, "rows", 0, 0, tiled=True)
    slots, *squares = own_work(
        coefficients, train_inputs, query_points, inv_length, block_inverse, factor_panel, row_count
    )
    own_queries = lax.dynamic_slice_in_dim(query_points, row_index * piece, piece, 1)
    solved, carried = solve(coefficients, arrived, squares)
    kernel = near(arrived, own_queries, inv_length, carried)
    carried = lax.ppermute(carried, "rows", [(1, 0)])
    weights, slots = correct(solved, carried, squares[0], squares[1], slots, kernel)
    pieces = lax.all_to_all(slots, "rows", 0, 0, tiled=True)
    return (weights, finish(pieces, kernel, amplitude))


def solution(mesh):
    return jax.shard_map(
        on_device,
        mesh=mesh,
        in_specs=(
            P("cols", "rows"),
            P("rows", None),
            P("rows", None),
            P(None, "rows"),
            P(),
            P(),
            P("cols"),
        ),
        out_specs=(P("cols", "rows"), P("cols", "rows")),
        check_vma=False,
    )
```

```python
import functools
import math

import jax
import jax.numpy as jnp
from jax import lax
from jax.experimental import pallas as pl
from jax.experimental.pallas import tpu as pltpu
from jax.sharding import PartitionSpec as P

F32 = jnp.float32
BF16 = jnp.bfloat16
LOG2E = math.log2(math.e)
FLOOR = 1e-06 * LOG2E * LOG2E
PADDED = 16
WHOLE = pl.BlockSpec(memory_space=pltpu.VMEM)
SCALARS = pl.BlockSpec(memory_space=pltpu.SMEM)
UNREAD = pl.BlockSpec(memory_space=pl.ANY)
PARAMS = pltpu.CompilerParams(vmem_limit_bytes=16 * 1024 * 1024)
ALONE = pltpu.CompilerParams(vmem_limit_bytes=56 * 1024 * 1024)
LINES = range(1, 4)

def split(values):
    high = values.astype(BF16)
    return high, (values - high.astype(F32)).astype(BF16)


def dot(left, right):
    return jnp.dot(left, right, preferred_element_type=F32)


def product(left, right_high, right_low):
    rows = left.shape[0]
    left_high, left_low = split(left)
    both = dot(jnp.concatenate([left_high, left_low], axis=0), right_high)
    return both[:rows] + both[rows:] + dot(left_high, right_low)


def three_pieces(values):
    high = values.astype(BF16).astype(F32)
    rest = values - high
    middle = rest.astype(BF16).astype(F32)
    low = (rest - middle).astype(BF16).astype(F32)
    return high, middle, low


def extra_rows(rows, count):
    width = rows[0].shape[1]
    index = lax.broadcasted_iota(jnp.int32, (count, width), 0)
    block = jnp.zeros((count, width), F32)
    for place, row in enumerate(rows):
        block = jnp.where(index == place, jnp.broadcast_to(row, (count, width)), block)
    return block


def train_side(points):
    norm = jnp.sum(points * points, axis=0, keepdims=True)
    high, middle, low = (-2.0 * piece for piece in three_pieces(points))
    one = jnp.ones_like(norm)
    extra = extra_rows([one, one, one, *three_pieces(norm)], 32)
    left = jnp.concatenate([high, middle, low, high, middle, high, extra], axis=0)
    return left.T.astype(BF16)


def query_side(points):
    norm = jnp.sum(points * points, axis=0, keepdims=True)
    high, middle, low = three_pieces(points)
    one = jnp.ones_like(norm)
    extra = extra_rows([*three_pieces(norm), one, one, one], 32)
    right = jnp.concatenate([high, high, high, middle, middle, low, extra], axis=0)
    return right.astype(BF16)


def kernel_values(left, right):
    squared = jnp.maximum(dot(left, right), 0.0) + FLOOR
    return jnp.exp2(-(squared * lax.rsqrt(squared))).astype(BF16)


def scale_column(inv_length_ref):
    index = lax.broadcasted_iota(jnp.int32, (PADDED, 1), 0)
    column = jnp.zeros((PADDED, 1), F32)
    for place in range(inv_length_ref.shape[0]):
        column = jnp.where(index == place, inv_length_ref[place] * LOG2E, column)
    return column


def centred(pad_ref, points):
    pad_ref[...] = jnp.zeros_like(pad_ref)
    pad_ref[: points.shape[0], :] = points - 0.5
    return pad_ref[...]


def position():
    row_index = lax.axis_index("rows")
    return row_index, row_index // 4, row_index % 4


def residual_kernel(coefficients_ref, factor_ref, out_ref, left_ref, stage_ref, sems):
    row_index, _, _ = position()
    parts, depth, _ = stage_ref.shape

    @pl.when(row_index >= 2)
    def _():
        first = pltpu.make_async_copy(coefficients_ref, left_ref, sems.at[parts])
        first.start()
        copies = [
            pltpu.make_async_copy(
                factor_ref.at[part * depth : (part + 1) * depth, :], stage_ref.at[part], sems.at[part]
            )
            for part in range(parts)
        ]
        for copy in copies:
            copy.start()
        first.wait()
        partial = jnp.zeros(out_ref.shape, F32)
        for part, copy in enumerate(copies):
            left = left_ref[:, part * depth : (part + 1) * depth]
            copy.wait()
            partial = partial + product(left, *split(stage_ref[part]))
        out_ref[...] = partial.astype(BF16)

    @pl.when(row_index < 2)
    def _():
        out_ref[...] = jnp.zeros_like(out_ref)


def residuals(coefficients, factor_panel):
    rows, block_len = coefficients.shape
    parts = 4
    return pl.pallas_call(
        residual_kernel,
        out_shape=jax.ShapeDtypeStruct((rows, 2 * block_len), BF16),
        in_specs=[UNREAD, UNREAD],
        out_specs=WHOLE,
        scratch_shapes=[
            pltpu.VMEM((rows, block_len), F32),
            pltpu.VMEM((parts, block_len // parts, 2 * block_len), F32),
            pltpu.SemaphoreType.DMA((parts + 1,)),
        ],
        compiler_params=ALONE,
        name="residuals",
    )(coefficients, factor_panel)


def combine_kernel(own_ref, first_ref, second_ref, third_ref, sum_ref, *send_refs):
    _, line, place = position()
    block_len = sum_ref.shape[1]

    @pl.when(line == 0)
    def _():
        total = own_ref[...].astype(F32) + first_ref[...].astype(F32)
        total = total + second_ref[...].astype(F32) + third_ref[...].astype(F32)
        for_zero, for_one = total[:, :block_len], total[:, block_len:]
        sum_ref[...] = jnp.where(place == 1, for_one, for_zero)
        for sender, send_ref in zip((0, 2, 3), send_refs):
            send_ref[...] = jnp.where(place == sender, for_one, for_zero).astype(BF16)

    @pl.when(line > 0)
    def _():
        sum_ref[...] = jnp.zeros_like(sum_ref)
        for send_ref in send_refs:
            send_ref[...] = jnp.zeros_like(send_ref)


def combine(own, arrived):
    rows, width = own.shape
    half = (rows, width // 2)
    return pl.pallas_call(
        combine_kernel,
        out_shape=(jax.ShapeDtypeStruct(half, F32),) + (jax.ShapeDtypeStruct(half, BF16),) * 3,
        in_specs=[WHOLE] * 4,
        out_specs=(WHOLE,) * 4,
        compiler_params=PARAMS,
        name="combine",
    )(own, *arrived)


def own_kernel(
    coefficients_ref, train_ref, query_ref, inv_length_ref, _, out_ref, points_ref, left_ref, pad_ref, pad_query_ref
):
    row_index, _, _ = position()
    count, _, piece = out_ref.shape

    @pl.when(row_index < 2)
    def _():
        points_ref[...] = jnp.concatenate(split(centred(pad_ref, train_ref[...])), axis=0)

    @pl.when(row_index >= 2)
    def _():
        scale = scale_column(inv_length_ref)
        left_ref[...] = train_side(centred(pad_ref, train_ref[...]) * scale)
        low = coefficients_ref[...].astype(BF16)

        length = pad_query_ref.shape[1]
        places = length // piece

        def step(part, carry):
            chosen = query_ref[:, pl.ds(pl.multiple_of(part * length, length), length)]
            right = query_side(centred(pad_query_ref, chosen) * scale)
            terms = dot(low, kernel_values(left_ref[...], right)).astype(BF16)
            for place in range(places):
                out_ref[part * places + place] = terms[:, place * piece : (place + 1) * piece]
            return carry

        lax.fori_loop(0, count // places, step, 0)


def own_work(coefficients, train_inputs, query_points, inv_length, row_count, unread):
    rows, plans = coefficients.shape
    queries = query_points.shape[1]
    piece = queries // row_count
    return pl.pallas_call(
        own_kernel,
        out_shape=(
            jax.ShapeDtypeStruct((row_count, rows, piece), BF16),
            jax.ShapeDtypeStruct((2 * PADDED, plans), BF16),
        ),
        in_specs=[WHOLE, WHOLE, WHOLE, SCALARS, UNREAD],
        out_specs=(WHOLE, WHOLE),
        scratch_shapes=[
            pltpu.VMEM((plans, 128), BF16),
            pltpu.VMEM((PADDED, plans), F32),
            pltpu.VMEM((PADDED, 4 * piece), F32),
        ],
        compiler_params=pltpu.CompilerParams(vmem_limit_bytes=24 * 1024 * 1024),
        cost_estimate=pl.CostEstimate(
            flops=2 * 160 * plans * queries, bytes_accessed=1 << 20, transcendentals=2 * plans * queries
        ),
        name="own_work",
    )(coefficients, train_inputs, query_points, inv_length, unread)


def solve_kernel(
    coefficients_ref, sum_ref, first_ref, second_ref, third_ref, inverse_ref, factor_ref,
    points_ref, points_one_ref, points_two_ref, points_three_ref, out_ref, send_ref, held_ref,
):
    row_index, line, _ = position()

    @pl.when(row_index < 2)
    def _():
        total = sum_ref[...] + first_ref[...].astype(F32)
        total = total + second_ref[...].astype(F32) + third_ref[...].astype(F32)
        out_ref[...] = product(coefficients_ref[...] - total, *split(inverse_ref[...]))

    @pl.when(row_index == 1)
    def _():
        send_ref[...] = product(out_ref[...], *split(factor_ref[...])).astype(BF16)

    @pl.when(row_index >= 2)
    def _():
        out_ref[...] = coefficients_ref[...]

    @pl.when(line == 0)
    def _():
        held_ref[...] = points_ref[...]

    for step, arrived_ref in zip(LINES, (points_one_ref, points_two_ref, points_three_ref)):

        @pl.when(line == step)
        def _():
            held_ref[...] = arrived_ref[...]


def solve(coefficients, total, arrived, block_inverse, factor_panel, points):
    rows, block_len = coefficients.shape
    small = pl.BlockSpec((rows, block_len), lambda j: (0, 0))
    square = pl.BlockSpec((block_len, block_len), lambda j: (0, 0))
    pair = pl.BlockSpec(points[0].shape, lambda j: (0, 0))
    return pl.pallas_call(
        solve_kernel,
        out_shape=(
            jax.ShapeDtypeStruct((rows, block_len), F32),
            jax.ShapeDtypeStruct((rows, block_len), BF16),
            jax.ShapeDtypeStruct(points[0].shape, BF16),
        ),
        grid=(1,),
        in_specs=[small] * 5 + [square, square] + [pair] * 4,
        out_specs=(small, small, pair),
        compiler_params=PARAMS,
        name="solve",
    )(coefficients, total, *arrived, block_inverse, factor_panel, *points)


def correct_kernel(solved_ref, carried_ref, inverse_ref, own_ref, points_ref, out_ref, slots_ref, held_ref):
    row_index, _, _ = position()
    held_ref[...] = points_ref[...]

    @pl.when(row_index == 0)
    def _():
        high, low = split(inverse_ref[...])
        carried = carried_ref[...]
        out_ref[...] = solved_ref[...] - (dot(carried, high) + dot(carried, low))

    @pl.when(row_index > 0)
    def _():
        out_ref[...] = solved_ref[...]

    @pl.when(row_index < 2)
    def _():
        low = out_ref[...].astype(BF16)
        for slot in range(slots_ref.shape[0]):
            slots_ref[slot] = low

    @pl.when(row_index >= 2)
    def _():
        slots_ref[...] = own_ref[...]


def correct(solved, carried, block_inverse, own, points):
    return pl.pallas_call(
        correct_kernel,
        out_shape=(
            jax.ShapeDtypeStruct(solved.shape, F32),
            jax.ShapeDtypeStruct(own.shape, own.dtype),
            jax.ShapeDtypeStruct(points.shape, points.dtype),
        ),
        in_specs=[WHOLE] * 5,
        out_specs=(WHOLE,) * 3,
        compiler_params=PARAMS,
        name="correct",
    )(solved, carried, block_inverse, own, points)


def near_kernel(own_ref, first_ref, second_ref, third_ref, query_ref, inv_length_ref, kernel_ref, pad_ref):
    _, _, place = position()
    scale = scale_column(inv_length_ref)
    right = query_side(centred(pad_ref, query_ref[...]) * scale)
    plans = own_ref.shape[1]
    own, first, second, third = (ref[...].astype(F32) for ref in (own_ref, first_ref, second_ref, third_ref))
    zero = jnp.where(place == 0, own, jnp.where(place == 1, first, jnp.where(place == 2, second, third)))
    one = jnp.where(place == 1, own, jnp.where(place == 0, first, jnp.where(place == 3, second, third)))
    for block, both in enumerate((zero, one)):
        left = train_side((both[:PADDED] + both[PADDED:]) * scale)
        kernel_ref[block * plans : (block + 1) * plans, :] = kernel_values(left, right)


def near(own, arrived, own_queries, inv_length):
    plans, queries = own.shape[1], own_queries.shape[1]
    return pl.pallas_call(
        near_kernel,
        out_shape=jax.ShapeDtypeStruct((2 * plans, queries), BF16),
        in_specs=[WHOLE] * 5 + [SCALARS],
        out_specs=WHOLE,
        scratch_shapes=[pltpu.VMEM((PADDED, queries), F32)],
        compiler_params=PARAMS,
        cost_estimate=pl.CostEstimate(
            flops=4 * 128 * plans * queries, bytes_accessed=1 << 20, transcendentals=4 * plans * queries
        ),
        name="near",
    )(own, *arrived, own_queries, inv_length)


def finish_kernel(pieces_ref, kernel_ref, amplitude_ref, mean_ref):
    rows = mean_ref.shape[0]
    plans = kernel_ref.shape[0] // 2
    mean = jnp.sum(pieces_ref[2:].astype(F32), axis=0)
    mean = mean + dot(pieces_ref[0], kernel_ref[:plans, :]) + dot(pieces_ref[1], kernel_ref[plans:, :])
    index = lax.broadcasted_iota(jnp.int32, (rows, 1), 0)
    amplitude = jnp.zeros((rows, 1), F32)
    for row in range(rows):
        amplitude = jnp.where(index == row, amplitude_ref[row], amplitude)
    mean_ref[...] = mean * amplitude


def finish(pieces, kernel, amplitude):
    return pl.pallas_call(
        finish_kernel,
        out_shape=jax.ShapeDtypeStruct(pieces.shape[1:], F32),
        in_specs=[WHOLE, WHOLE, SCALARS],
        out_specs=WHOLE,
        compiler_params=PARAMS,
        name="finish",
    )(pieces, kernel, amplitude)


def on_device(
    coefficients, factor_panel, block_inverse, train_inputs, query_points, inv_length, amplitude
):
    row_index = lax.axis_index("rows")
    row_count = lax.axis_size("rows")
    piece = query_points.shape[1] // row_count
    gathers = (((0, 1), (1, 0)), ((2, 1), (3, 0)), ((3, 1), (2, 0)))
    spreads = (((0, 1), (1, 0)), ((0, 2), (1, 3)), ((0, 3), (1, 2)))

    partial = residuals(coefficients, factor_panel)
    arrived = [lax.ppermute(partial, "rows", [(4 * x + z, z) for z in range(4)]) for x in LINES]
    total, *sends = combine(partial, arrived)
    arrived = [lax.ppermute(send, "rows", pairs) for send, pairs in zip(sends, gathers)]
    own, points = own_work(coefficients, train_inputs, query_points, inv_length, row_count, sends[0])
    points = [points, *(lax.ppermute(points, "rows", [(0, 4 * x), (1, 4 * x + 1)]) for x in LINES)]
    solved, carried, points = solve(coefficients, total, arrived, block_inverse, factor_panel, points)

    carried = lax.ppermute(carried, "rows", [(1, 0)])
    weights, slots, points = correct(solved, carried, block_inverse, own, points)
    pieces = lax.all_to_all(slots, "rows", 0, 0, tiled=True)

    along = [
        lax.ppermute(points, "rows", [(4 * x + a, 4 * x + b) for x in range(4) for a, b in pairs])
        for pairs in spreads
    ]
    own_queries = lax.dynamic_slice_in_dim(query_points, row_index * piece, piece, 1)
    kernel = near(points, along, own_queries, inv_length)
    return (weights, finish(pieces, kernel, amplitude))


def solution(mesh):
    return jax.shard_map(
        on_device,
        mesh=mesh,
        in_specs=(
            P("cols", "rows"),
            P("rows", None),
            P("rows", None),
            P(None, "rows"),
            P(),
            P(),
            P("cols"),
        ),
        out_specs=(P("cols", "rows"), P("cols", "rows")),
        check_vma=False,
    )
```

```python
import functools
import math

import jax
import jax.numpy as jnp
from jax import lax
from jax.experimental import pallas as pl
from jax.experimental.pallas import tpu as pltpu
from jax.sharding import PartitionSpec as P

F32 = jnp.float32
BF16 = jnp.bfloat16
LOG2E = math.log2(math.e)
FLOOR = 1e-06 * LOG2E * LOG2E
PADDED = 16
WHOLE = pl.BlockSpec(memory_space=pltpu.VMEM)
SCALARS = pl.BlockSpec(memory_space=pltpu.SMEM)
UNREAD = pl.BlockSpec(memory_space=pl.ANY)
PARAMS = pltpu.CompilerParams(vmem_limit_bytes=16 * 1024 * 1024)
ALONE = pltpu.CompilerParams(vmem_limit_bytes=56 * 1024 * 1024)
LINES = range(1, 4)

def split(values):
    high = values.astype(BF16)
    return high, (values - high.astype(F32)).astype(BF16)


def dot(left, right):
    return jnp.dot(left, right, preferred_element_type=F32)


def product(left, right_high, right_low):
    rows = left.shape[0]
    left_high, left_low = split(left)
    both = dot(jnp.concatenate([left_high, left_low], axis=0), right_high)
    return both[:rows] + both[rows:] + dot(left_high, right_low)


def three_pieces(values):
    high = values.astype(BF16).astype(F32)
    rest = values - high
    middle = rest.astype(BF16).astype(F32)
    low = (rest - middle).astype(BF16).astype(F32)
    return high, middle, low


def extra_rows(rows, count):
    width = rows[0].shape[1]
    index = lax.broadcasted_iota(jnp.int32, (count, width), 0)
    block = jnp.zeros((count, width), F32)
    for place, row in enumerate(rows):
        block = jnp.where(index == place, jnp.broadcast_to(row, (count, width)), block)
    return block


def train_side(points):
    norm = jnp.sum(points * points, axis=0, keepdims=True)
    high, middle, low = (-2.0 * piece for piece in three_pieces(points))
    one = jnp.ones_like(norm)
    extra = extra_rows([one, one, one, *three_pieces(norm)], 32)
    left = jnp.concatenate([high, middle, low, high, middle, high, extra], axis=0)
    return left.T.astype(BF16)


def query_side(points):
    norm = jnp.sum(points * points, axis=0, keepdims=True)
    high, middle, low = three_pieces(points)
    one = jnp.ones_like(norm)
    extra = extra_rows([*three_pieces(norm), one, one, one], 32)
    right = jnp.concatenate([high, high, high, middle, middle, low, extra], axis=0)
    return right.astype(BF16)


def kernel_values(left, right):
    squared = jnp.maximum(dot(left, right), 0.0) + FLOOR
    return jnp.exp2(-(squared * lax.rsqrt(squared))).astype(BF16)


def scale_column(inv_length_ref):
    index = lax.broadcasted_iota(jnp.int32, (PADDED, 1), 0)
    column = jnp.zeros((PADDED, 1), F32)
    for place in range(inv_length_ref.shape[0]):
        column = jnp.where(index == place, inv_length_ref[place] * LOG2E, column)
    return column


def centred(pad_ref, points):
    pad_ref[...] = jnp.zeros_like(pad_ref)
    pad_ref[: points.shape[0], :] = points - 0.5
    return pad_ref[...]


def position():
    row_index = lax.axis_index("rows")
    return row_index, row_index // 4, row_index % 4


def residual_kernel(coefficients_ref, factor_ref, out_ref, left_ref, stage_ref, sems):
    row_index, _, _ = position()
    parts, depth, _ = stage_ref.shape

    @pl.when(row_index >= 2)
    def _():
        first = pltpu.make_async_copy(coefficients_ref, left_ref, sems.at[parts])
        first.start()
        copies = [
            pltpu.make_async_copy(
                factor_ref.at[part * depth : (part + 1) * depth, :], stage_ref.at[part], sems.at[part]
            )
            for part in range(parts)
        ]
        for copy in copies:
            copy.start()
        first.wait()
        partial = jnp.zeros(out_ref.shape, F32)
        for part, copy in enumerate(copies):
            left = left_ref[:, part * depth : (part + 1) * depth]
            copy.wait()
            partial = partial + product(left, *split(stage_ref[part]))
        out_ref[...] = partial.astype(BF16)

    @pl.when(row_index < 2)
    def _():
        out_ref[...] = jnp.zeros_like(out_ref)


def residuals(coefficients, factor_panel):
    rows, block_len = coefficients.shape
    parts = 4
    return pl.pallas_call(
        residual_kernel,
        out_shape=jax.ShapeDtypeStruct((rows, 2 * block_len), BF16),
        in_specs=[UNREAD, UNREAD],
        out_specs=WHOLE,
        scratch_shapes=[
            pltpu.VMEM((rows, block_len), F32),
            pltpu.VMEM((parts, block_len // parts, 2 * block_len), F32),
            pltpu.SemaphoreType.DMA((parts + 1,)),
        ],
        compiler_params=ALONE,
        name="residuals",
    )(coefficients, factor_panel)


def combine_kernel(own_ref, first_ref, second_ref, third_ref, sum_ref, *refs):
    send_refs, (mine_ref, sem) = refs[:3], refs[3:]
    _, line, place = position()
    block_len = sum_ref.shape[1]

    @pl.when(line == 0)
    def _():
        copy = pltpu.make_async_copy(own_ref, mine_ref, sem.at[0])
        copy.start()
        total = first_ref[...].astype(F32) + second_ref[...].astype(F32) + third_ref[...].astype(F32)
        copy.wait()
        total = total + mine_ref[...].astype(F32)
        for_zero, for_one = total[:, :block_len], total[:, block_len:]
        sum_ref[...] = jnp.where(place == 1, for_one, for_zero)
        for sender, send_ref in zip((0, 2, 3), send_refs):
            send_ref[...] = jnp.where(place == sender, for_one, for_zero).astype(BF16)

    @pl.when(line > 0)
    def _():
        sum_ref[...] = jnp.zeros_like(sum_ref)
        for send_ref in send_refs:
            send_ref[...] = jnp.zeros_like(send_ref)


def combine(own, arrived):
    rows, width = own.shape
    half = (rows, width // 2)
    return pl.pallas_call(
        combine_kernel,
        out_shape=(jax.ShapeDtypeStruct(half, F32),) + (jax.ShapeDtypeStruct(half, BF16),) * 3,
        in_specs=[UNREAD] + [WHOLE] * 3,
        out_specs=(WHOLE,) * 4,
        scratch_shapes=[pltpu.VMEM((rows, width), BF16), pltpu.SemaphoreType.DMA((1,))],
        compiler_params=PARAMS,
        name="combine",
    )(own, *arrived)


def own_kernel(
    coefficients_ref, train_ref, query_ref, inv_length_ref, _, out_ref, points_ref, left_ref, pad_ref, pad_query_ref
):
    row_index, _, _ = position()
    count, _, piece = out_ref.shape

    @pl.when(row_index < 2)
    def _():
        points_ref[...] = jnp.concatenate(split(centred(pad_ref, train_ref[...])), axis=0)

    @pl.when(row_index >= 2)
    def _():
        scale = scale_column(inv_length_ref)
        left_ref[...] = train_side(centred(pad_ref, train_ref[...]) * scale)
        low = coefficients_ref[...].astype(BF16)

        length = pad_query_ref.shape[1]
        places = length // piece

        def step(part, carry):
            chosen = query_ref[:, pl.ds(pl.multiple_of(part * length, length), length)]
            right = query_side(centred(pad_query_ref, chosen) * scale)
            terms = dot(low, kernel_values(left_ref[...], right)).astype(BF16)
            for place in range(places):
                out_ref[part * places + place] = terms[:, place * piece : (place + 1) * piece]
            return carry

        lax.fori_loop(0, count // places, step, 0)


def own_work(coefficients, train_inputs, query_points, inv_length, row_count, unread):
    rows, plans = coefficients.shape
    queries = query_points.shape[1]
    piece = queries // row_count
    return pl.pallas_call(
        own_kernel,
        out_shape=(
            jax.ShapeDtypeStruct((row_count, rows, piece), BF16),
            jax.ShapeDtypeStruct((2 * PADDED, plans), BF16),
        ),
        in_specs=[WHOLE, WHOLE, WHOLE, SCALARS, UNREAD],
        out_specs=(WHOLE, WHOLE),
        scratch_shapes=[
            pltpu.VMEM((plans, 128), BF16),
            pltpu.VMEM((PADDED, plans), F32),
            pltpu.VMEM((PADDED, 4 * piece), F32),
        ],
        compiler_params=pltpu.CompilerParams(vmem_limit_bytes=24 * 1024 * 1024),
        cost_estimate=pl.CostEstimate(
            flops=2 * 160 * plans * queries, bytes_accessed=1 << 20, transcendentals=2 * plans * queries
        ),
        name="own_work",
    )(coefficients, train_inputs, query_points, inv_length, unread)


def solve_kernel(
    coefficients_ref, sum_ref, first_ref, second_ref, third_ref, inverse_ref, factor_ref,
    points_ref, points_one_ref, points_two_ref, points_three_ref, out_ref, send_ref, held_ref,
):
    row_index, line, _ = position()

    @pl.when(row_index < 2)
    def _():
        total = sum_ref[...] + first_ref[...].astype(F32)
        total = total + second_ref[...].astype(F32) + third_ref[...].astype(F32)
        out_ref[...] = product(coefficients_ref[...] - total, *split(inverse_ref[...]))

    @pl.when(row_index == 1)
    def _():
        send_ref[...] = product(out_ref[...], *split(factor_ref[...])).astype(BF16)

    @pl.when(row_index >= 2)
    def _():
        out_ref[...] = coefficients_ref[...]

    @pl.when(line == 0)
    def _():
        held_ref[...] = points_ref[...]

    for step, arrived_ref in zip(LINES, (points_one_ref, points_two_ref, points_three_ref)):

        @pl.when(line == step)
        def _():
            held_ref[...] = arrived_ref[...]


def solve(coefficients, total, arrived, block_inverse, factor_panel, points):
    rows, block_len = coefficients.shape
    small = pl.BlockSpec((rows, block_len), lambda j: (0, 0))
    square = pl.BlockSpec((block_len, block_len), lambda j: (0, 0))
    pair = pl.BlockSpec(points[0].shape, lambda j: (0, 0))
    return pl.pallas_call(
        solve_kernel,
        out_shape=(
            jax.ShapeDtypeStruct((rows, block_len), F32),
            jax.ShapeDtypeStruct((rows, block_len), BF16),
            jax.ShapeDtypeStruct(points[0].shape, BF16),
        ),
        grid=(1,),
        in_specs=[small] * 5 + [square, square] + [pair] * 4,
        out_specs=(small, small, pair),
        compiler_params=PARAMS,
        name="solve",
    )(coefficients, total, *arrived, block_inverse, factor_panel, *points)


def correct_kernel(solved_ref, carried_ref, inverse_ref, own_ref, points_ref, out_ref, slots_ref, held_ref):
    row_index, _, _ = position()
    held_ref[...] = points_ref[...]

    @pl.when(row_index == 0)
    def _():
        high, low = split(inverse_ref[...])
        carried = carried_ref[...]
        out_ref[...] = solved_ref[...] - (dot(carried, high) + dot(carried, low))

    @pl.when(row_index > 0)
    def _():
        out_ref[...] = solved_ref[...]

    @pl.when(row_index < 2)
    def _():
        low = out_ref[...].astype(BF16)
        for slot in range(slots_ref.shape[0]):
            slots_ref[slot] = low

    @pl.when(row_index >= 2)
    def _():
        slots_ref[...] = own_ref[...]


def correct(solved, carried, block_inverse, own, points):
    return pl.pallas_call(
        correct_kernel,
        out_shape=(
            jax.ShapeDtypeStruct(solved.shape, F32),
            jax.ShapeDtypeStruct(own.shape, own.dtype),
            jax.ShapeDtypeStruct(points.shape, points.dtype),
        ),
        in_specs=[WHOLE] * 5,
        out_specs=(WHOLE,) * 3,
        compiler_params=PARAMS,
        name="correct",
    )(solved, carried, block_inverse, own, points)


def near_kernel(own_ref, first_ref, second_ref, third_ref, query_ref, inv_length_ref, kernel_ref, pad_ref):
    _, _, place = position()
    scale = scale_column(inv_length_ref)
    right = query_side(centred(pad_ref, query_ref[...]) * scale)
    plans = own_ref.shape[1]
    own, first, second, third = (ref[...].astype(F32) for ref in (own_ref, first_ref, second_ref, third_ref))
    zero = jnp.where(place == 0, own, jnp.where(place == 1, first, jnp.where(place == 2, second, third)))
    one = jnp.where(place == 1, own, jnp.where(place == 0, first, jnp.where(place == 3, second, third)))
    for block, both in enumerate((zero, one)):
        left = train_side((both[:PADDED] + both[PADDED:]) * scale)
        kernel_ref[block * plans : (block + 1) * plans, :] = kernel_values(left, right)


def near(own, arrived, own_queries, inv_length):
    plans, queries = own.shape[1], own_queries.shape[1]
    return pl.pallas_call(
        near_kernel,
        out_shape=jax.ShapeDtypeStruct((2 * plans, queries), BF16),
        in_specs=[WHOLE] * 5 + [SCALARS],
        out_specs=WHOLE,
        scratch_shapes=[pltpu.VMEM((PADDED, queries), F32)],
        compiler_params=PARAMS,
        cost_estimate=pl.CostEstimate(
            flops=4 * 128 * plans * queries, bytes_accessed=1 << 20, transcendentals=4 * plans * queries
        ),
        name="near",
    )(own, *arrived, own_queries, inv_length)


def finish_kernel(pieces_ref, kernel_ref, amplitude_ref, mean_ref):
    rows = mean_ref.shape[0]
    plans = kernel_ref.shape[0] // 2
    mean = jnp.sum(pieces_ref[2:].astype(F32), axis=0)
    mean = mean + dot(pieces_ref[0], kernel_ref[:plans, :]) + dot(pieces_ref[1], kernel_ref[plans:, :])
    index = lax.broadcasted_iota(jnp.int32, (rows, 1), 0)
    amplitude = jnp.zeros((rows, 1), F32)
    for row in range(rows):
        amplitude = jnp.where(index == row, amplitude_ref[row], amplitude)
    mean_ref[...] = mean * amplitude


def finish(pieces, kernel, amplitude):
    return pl.pallas_call(
        finish_kernel,
        out_shape=jax.ShapeDtypeStruct(pieces.shape[1:], F32),
        in_specs=[WHOLE, WHOLE, SCALARS],
        out_specs=WHOLE,
        compiler_params=PARAMS,
        name="finish",
    )(pieces, kernel, amplitude)


def on_device(
    coefficients, factor_panel, block_inverse, train_inputs, query_points, inv_length, amplitude
):
    row_index = lax.axis_index("rows")
    row_count = lax.axis_size("rows")
    piece = query_points.shape[1] // row_count
    gathers = (((0, 1), (1, 0)), ((2, 1), (3, 0)), ((3, 1), (2, 0)))
    spreads = (((0, 3), (1, 2)), ((0, 2), (1, 3)), ((0, 1), (1, 0)))

    partial = residuals(coefficients, factor_panel)
    arrived = [lax.ppermute(partial, "rows", [(4 * x + z, z) for z in range(4)]) for x in LINES]
    total, *sends = combine(partial, arrived)
    arrived = [lax.ppermute(send, "rows", pairs) for send, pairs in zip(sends, gathers)]
    own, points = own_work(coefficients, train_inputs, query_points, inv_length, row_count, sends[0])
    points = [points, *(lax.ppermute(points, "rows", [(0, 4 * x), (1, 4 * x + 1)]) for x in LINES)]
    solved, carried, points = solve(coefficients, total, arrived, block_inverse, factor_panel, points)

    carried = lax.ppermute(carried, "rows", [(1, 0)])
    weights, slots, points = correct(solved, carried, block_inverse, own, points)
    pieces = lax.all_to_all(slots, "rows", 0, 0, tiled=True)

    along = [
        lax.ppermute(points, "rows", [(4 * x + a, 4 * x + b) for x in range(4) for a, b in pairs])
        for pairs in spreads
    ]
    own_queries = lax.dynamic_slice_in_dim(query_points, row_index * piece, piece, 1)
    kernel = near(points, along[::-1], own_queries, inv_length)
    return (weights, finish(pieces, kernel, amplitude))


def solution(mesh):
    return jax.shard_map(
        on_device,
        mesh=mesh,
        in_specs=(
            P("cols", "rows"),
            P("rows", None),
            P("rows", None),
            P(None, "rows"),
            P(),
            P(),
            P("cols"),
        ),
        out_specs=(P("cols", "rows"), P("cols", "rows")),
        check_vma=False,
    )
```
